32 devices in a mesh: ao: 8 (over y, x, core), aux: 4 (over z).
Axes of the slice: x: 2, y: 2, z: 4, core: 2. Of those that a mesh axis runs over, the one named last changes fastest.
Arguments:
- factors: bfloat16 [16, 32, 256, 512], P('ao', 'aux'), may hold values from -0.8984375 to 0.8984375
- pair_cols: int32 [16, 3], P('ao'), may hold values from 0 to 15, as said below
- pair_count: int32 [16], P('ao'), may hold values from 1 to 3, as said below
Outputs:
- ex_blocks: float32 [16, 3, 256, 256], P('ao', None, 'aux')
The draws below stay inside these ranges and needn't reach their ends.
Inputs may be any that keep to these rules, and one draw needn't show every extreme that they name: pair_cols[a, s] = (a + t) mod 16 with 0 <= t < 7, the offsets t of one row all distinct; so every unordered pair of blocks stands at most once in the table. Slots at or beyond pair_count of a row are not live; some row is full.
All inputs are finite; a program needn't handle non-finite values.
Results may differ from the reference program's by a relative error of at most 0.0003.
Values may be sent and summed in bfloat16 or wider, within the bound.
No kernel may reach another device: no remote copies, remote signals or barrier semaphores. Data moves between devices by JAX's collectives and lax.ppermute only.
A program may use at most 320 MiB of HBM per device.

```python
import jax
import jax.numpy as jnp
from jax import lax

BS = 256
OCC = 512
NBLK = 16
AUXC = 32
HALF = 7
SLOTS = 3


def shuffled(key):
    return jax.random.permutation(key, HALF)[:SLOTS]


def draw_pair_cols(key, part):
    key = jax.random.fold_in(key, 11)
    row_keys = jax.random.split(key, NBLK)
    offsets = jax.vmap(shuffled)(row_keys).astype(jnp.int32)
    row_ids = jnp.arange(NBLK, dtype=jnp.int32)[:, None]
    return jnp.mod(row_ids + offsets, NBLK).astype(jnp.int32)


def draw_pair_count(key, part):
    key = jax.random.fold_in(key, 23)
    count_key, full_key = jax.random.split(key)
    lowest = max(1, (SLOTS + 2) // 3)
    counts = jax.random.randint(count_key, (NBLK,), lowest, SLOTS + 1)
    fullest = jax.random.randint(full_key, (), 0, NBLK)
    counts = jnp.where(jnp.arange(NBLK) == fullest, SLOTS, counts)
    return counts.astype(jnp.int32)


def level_of(stream_key, dims, shards, least, largest):
    def one(position, parts):
        steps = jax.random.uniform(jax.random.fold_in(jax.random.fold_in(stream_key, 6), position), (parts,), jnp.float32, least / len(shards), largest / len(shards))
        return jnp.repeat(jnp.exp(steps), dims[position] // parts).reshape((-1,) + (1,) * (len(dims) - position - 1))

    factor_of = one(*shards[0])
    for cut in shards[1:]:
        factor_of = factor_of * one(*cut)
    return factor_of


def gaussian(rng, shape, scale, reach, cuts=(), kind=jnp.bfloat16):
    array = jax.random.normal(rng, shape, jnp.float32) * scale
    if len(cuts) > 0:
        array = level_of(rng, shape, cuts, -0.22, 0.18) * array
    return jnp.clip(array, min=-reach, max=reach).astype(kind)


def setup_inputs(seed: int = 0) -> dict:
    keys = jax.random.split(jax.random.key(seed), 4)
    return {
        "factors": gaussian(keys[0], (NBLK, AUXC, BS, OCC), 0.15, 0.8984375, ((0, 8), (1, 4))),
        "pair_cols": draw_pair_cols(jax.random.fold_in(keys[3], 71), 0),
        "pair_count": draw_pair_count(jax.random.fold_in(keys[3], 71), 0),
    }


def reference(factors, pair_cols, pair_count):
    def one_row(row_index):
        row_slab = factors[row_index].astype(jnp.float32)
        col_slabs = jnp.take(factors, pair_cols[row_index].astype(jnp.int32), axis=0).astype(jnp.float32)
        product_block = jnp.einsum("pri,spci->src", row_slab, col_slabs)
        active = jnp.arange(SLOTS, dtype=jnp.int32) < pair_count[row_index]
        return jnp.where(active[:, None, None], product_block, jnp.zeros_like(product_block))

    return lax.map(one_row, jnp.arange(NBLK, dtype=jnp.int32))
```

```python
import functools

import jax
import jax.numpy as jnp
from jax import lax
from jax.experimental import pallas as pl
from jax.experimental.pallas import tpu as pltpu
from jax.sharding import PartitionSpec as P

LANES = 128
PIECES = ((0, 96), (96, 96), (192, 64))
GROUPS = 4
KERNEL_BYTES = 14 << 20


def pack_kernel(pieces, which, *refs):
    sources, outs, sems = refs[: -len(pieces) - 1], refs[-len(pieces) - 1 : -1], refs[-1]
    blocks = outs[0].shape[0]
    copies = [(turn, block) for turn in range(len(pieces)) for block in range(blocks)]

    def copy(source, turn, block):
        first, wide = pieces[turn]
        return pltpu.make_async_copy(
            source.at[block, :, pl.ds(first, wide)], outs[turn].at[block], sems.at[turn, block]
        )

    for index, source in enumerate(sources):

        @pl.when(which[0] == index)
        def start(source=source):
            for turn, block in copies:
                copy(source, turn, block).start()

    @pl.when(which[0] < len(sources))
    def wait():
        for turn, block in copies:
            copy(sources[0], turn, block).wait()


def in_hbm(value):
    return pltpu.with_memory_space_constraint(value, pltpu.HBM)


def pack(which, sources, pieces):
    blocks, depth, _, inner = sources[0].shape
    shapes = [jax.ShapeDtypeStruct((blocks, depth, wide, inner), sources[0].dtype) for _, wide in pieces]
    return pl.pallas_call(
        functools.partial(pack_kernel, pieces),
        in_specs=[pl.BlockSpec(memory_space=pltpu.SMEM)] + [pl.BlockSpec(memory_space=pl.ANY)] * len(sources),
        out_specs=[pl.BlockSpec(memory_space=pltpu.VMEM)] * len(pieces),
        scratch_shapes=[pltpu.SemaphoreType.DMA((len(pieces), blocks))],
        out_shape=shapes,
        compiler_params=pltpu.CompilerParams(vmem_limit_bytes=KERNEL_BYTES),
        cost_estimate=pl.CostEstimate(flops=0, bytes_accessed=1 << 20, transcendentals=0),
        name="pack_ranges",
    )(which, *sources)


def pair_kernel(slots, first, wide, parts, places, unread, rows_hbm, *refs):
    *refs, rows, held, total, row_sems, column_sems = refs
    sources, outs = refs[:-parts], refs[-parts:]
    blocks, depth, height, inner = rows.shape
    count = blocks * slots
    group = depth // GROUPS

    def row_copy(g):
        part = pl.ds(g * group, group)
        return pltpu.make_async_copy(rows_hbm.at[:, part], rows.at[:, part], row_sems.at[g])

    def column_copy(source, slot, g):
        part = pl.ds(g * group, group)
        start = first if source.shape[2] == height else 0
        return pltpu.make_async_copy(
            source.at[places[count + slot], part, pl.ds(start, wide)],
            held.at[slot // slots, part, pl.ds(slot % slots * wide, wide)],
            column_sems.at[slot, g],
        )

    for g in range(GROUPS):
        row_copy(g).start()
        for slot in range(count):
            for index, source in enumerate(sources):

                @pl.when(places[slot] == index)
                def fetch(source=source, slot=slot, g=g):
                    column_copy(source, slot, g).start()

    for g in range(GROUPS):
        row_copy(g).wait()
        for slot in range(count):

            @pl.when(places[slot] >= 0)
            def arrived(slot=slot, g=g):
                column_copy(sources[-1], slot, g).wait()

        for row in range(blocks):
            product = 0.0 if g == 0 else total[row]
            for p in range(g * group, (g + 1) * group):
                product += lax.dot_general(
                    held[row, p],
                    rows[row, p],
                    (((1,), (1,)), ((), ())),
                    preferred_element_type=jnp.float32,
                )
            total[row] = product

    parts = len(outs)
    lanes = outs[0].shape[2]
    span = height // parts
    fold = lanes // span
    for slot in range(count):
        start = slot % slots * wide
        block = jnp.where(places[slot] >= 0, total[slot // slots, start : start + wide], 0.0)
        left = slot % fold * span
        for mine in range(parts):

            @pl.when(places[2 * count] == mine)
            def write(slot=slot, block=block, left=left, mine=mine):
                for step, out in enumerate(outs):
                    part = (mine + step) % parts
                    out[slot // fold, :, left : left + span] = block[:, part * span : (part + 1) * span]


def pair_products(places, begun, rows, columns, piece, parts, slots):
    first, wide = piece
    blocks, depth, height, inner = rows.shape
    count = blocks * slots
    fold = LANES * parts // height if count % (LANES * parts // height) == 0 else 1
    shape = (count // fold, wide, height // parts * fold)
    return pl.pallas_call(
        functools.partial(pair_kernel, slots, first, wide, parts),
        in_specs=[pl.BlockSpec(memory_space=pltpu.SMEM)] + [pl.BlockSpec(memory_space=pl.ANY)]
        + [pl.BlockSpec(memory_space=pl.ANY)] * (1 + len(columns)),
        out_specs=[pl.BlockSpec(memory_space=pltpu.VMEM)] * parts,
        scratch_shapes=[
            pltpu.VMEM(rows.shape, rows.dtype),
            pltpu.VMEM((blocks, depth, slots * wide, inner), rows.dtype),
            pltpu.VMEM((blocks, slots * wide, height), jnp.float32),
            pltpu.SemaphoreType.DMA((GROUPS,)),
            pltpu.SemaphoreType.DMA((count, GROUPS)),
        ],
        out_shape=[jax.ShapeDtypeStruct(shape, jnp.float32)] * parts,
        compiler_params=pltpu.CompilerParams(vmem_limit_bytes=KERNEL_BYTES),
        cost_estimate=pl.CostEstimate(flops=0, bytes_accessed=1 << 20, transcendentals=0),
        name="pair_products",
    )(places, begun, *(in_hbm(a) if a.shape == rows.shape else a for a in (rows, *columns)))


def sum_kernel(parts, *refs):
    *terms, out = refs
    pairs, _, lanes = terms[0].shape
    span = out.shape[1]
    for pair in range(pairs):
        sums = [sum(term[pair] for term in terms[k : k + parts]) for k in range(0, len(terms), parts)]
        turned = jnp.concatenate(sums, axis=0).T
        for side in range(lanes // span):
            out[pair * (lanes // span) + side] = turned[side * span : (side + 1) * span]


def mark_kernel(value, out):
    out[...] = jnp.zeros_like(out)


def mark(value):
    return pl.pallas_call(
        mark_kernel,
        in_specs=[pl.BlockSpec(memory_space=pl.ANY)],
        out_specs=pl.BlockSpec(memory_space=pltpu.VMEM),
        out_shape=jax.ShapeDtypeStruct((8, LANES), jnp.float32),
        compiler_params=pltpu.CompilerParams(vmem_limit_bytes=1 << 20),
        cost_estimate=pl.CostEstimate(flops=10**12, bytes_accessed=10**9, transcendentals=0),
        name="mark",
    )(value)


def squares(factors, pair_cols, pair_count):
    blocks, _, height, _ = factors.shape
    slots = pair_cols.shape[1]
    devices = lax.axis_size("ao")
    parts = lax.axis_size("aux")
    chips = devices // 2
    me = lax.axis_index("ao")
    core = lax.rem(me, 2)
    even = lax.rem(me, 4) < 2

    swap = [(d, d ^ 1) for d in range(devices)]
    to_core_1 = [(2 * c, 2 * c + 1) for c in range(chips)]
    early, late = [], []
    for c in range(0, chips, 2):
        across = (c + 2) % chips
        early += [(2 * across, 2 * c), (2 * c + 3, 2 * c + 1), (2 * across + 1, 2 * c + 3)]
        late += [(2 * c, 2 * c + 2), (2 * c + 2, 2 * c), (2 * across + 3, 2 * c + 3)]

    relative = jnp.mod(pair_cols - me * blocks, devices * blocks)
    slab = relative // blocks
    first_core = jnp.where(slab == 2, 4, jnp.where(slab == 3, 3, slab))
    second_core = jnp.where(slab == 1, 5, jnp.where(slab == 2, 2, jnp.where(even, 3, 4)))
    source = jnp.where((core == 0) | (slab == 0), first_core, second_core)
    live = lax.broadcasted_iota(jnp.int32, (blocks, slots), 1) < pair_count[:, None]
    places = jnp.concatenate([jnp.where(live, source, -1).reshape(-1), lax.rem(relative, blocks).reshape(-1)])
    places = jnp.concatenate([places, lax.axis_index("aux").astype(jnp.int32).reshape(1)])
    which = jnp.where(even, 3 * core, 1 + core).astype(jnp.int32).reshape(1)

    one = lax.ppermute(factors, "ao", early)
    mate = lax.ppermute(factors, "ao", swap)
    one_mate = lax.ppermute(one, "ao", swap)
    senders = [one, in_hbm(factors), mate]
    sent = pack(which, senders, PIECES[:1])
    sent += pack(after(which, places, *sent), senders, PIECES[1:])
    twos, made, terms, marks = [], [], [], [mark(sent[-1])]
    for turn, piece in enumerate(PIECES):
        twos.append(lax.ppermute(after(sent[turn], *made[: max(turn - 1, 0)][-1:]), "ao", late))
        earlier = terms[1 - parts :] if turn == 1 else []
        two_mate = lax.ppermute(after(twos[turn], marks[turn], *earlier), "ao", to_core_1)
        columns = [factors, mate, one, one_mate, twos[turn], two_mate]
        products = pair_products(places, marks[turn], factors, columns, piece, parts, slots)
        made.append(products[0])
        if turn + 1 < len(PIECES):
            marks.append(mark(products[0]))
        terms.append(products[0])
        for step in range(1, parts):
            terms.append(lax.ppermute(products[step], "aux", [(z, (z + step) % parts) for z in range(parts)]))
    out = pl.pallas_call(
        functools.partial(sum_kernel, parts),
        out_shape=jax.ShapeDtypeStruct((blocks * slots, height // parts, height), jnp.float32),
        compiler_params=pltpu.CompilerParams(vmem_limit_bytes=KERNEL_BYTES),
        name="sum_terms",
    )(*terms)
    return out.reshape(blocks, slots, height // parts, height)


def after(value, *others):
    return lax.optimization_barrier((value, *others))[0]


def from_behind(value, axis, steps):
    count = lax.axis_size(axis)
    pairs = [(source, (source + steps) % count) for source in range(count)]
    return lax.ppermute(value, axis, pairs)


def ring(factors, pair_cols, pair_count):
    blocks_dev = factors.shape[0]
    slot_total = pair_cols.shape[1]
    devices = lax.axis_size("ao")

    def advance(carry, unused):
        arrived = from_behind(carry, "ao", -1)
        return (arrived, arrived)

    last_block, received = lax.scan(advance, factors, None, length=devices // 2 - 1)
    resident = jnp.concatenate([factors, received.reshape((-1,) + factors.shape[1:])], axis=0)
    offset = lax.axis_index("ao") * blocks_dev
    slot_index = jnp.mod(pair_cols - offset, devices * blocks_dev)
    columns = jnp.take(resident, slot_index.reshape(-1), axis=0)
    columns = columns.reshape((blocks_dev, slot_total) + factors.shape[1:])
    partial_value = jnp.einsum(
        "apri,aspci->asrc", factors, columns, preferred_element_type=jnp.float32
    )
    active = lax.broadcasted_iota(jnp.int32, (blocks_dev, slot_total), 1) < pair_count[:, None]
    partial_value = jnp.where(active[:, :, None, None], partial_value, 0.0)
    return lax.psum_scatter(partial_value, "aux", scatter_dimension=2, tiled=True)


def solution(mesh):
    return jax.shard_map(
        squares if mesh.shape["ao"] == 8 else ring,
        mesh=mesh,
        in_specs=(P("ao", "aux", None, None), P("ao", None), P("ao")),
        out_specs=P("ao", None, "aux", None),
        check_vma=False,
    )
```

```python
import functools

import jax
import jax.numpy as jnp
from jax import lax
from jax.experimental import pallas as pl
from jax.experimental.pallas import tpu as pltpu
from jax.sharding import PartitionSpec as P

LANES = 128
PIECES = ((0, 48), (48, 96), (144, 112))
GROUPS = 4
KERNEL_BYTES = 14 << 20
MARK_FLOPS = 10**6


def pack_kernel(pieces, which, *refs):
    sources, outs, sems = refs[: -len(pieces) - 1], refs[-len(pieces) - 1 : -1], refs[-1]
    blocks, depth = outs[0].shape[:2]
    group = depth // GROUPS
    copies = [(turn, block, g) for turn in range(len(pieces)) for block in range(blocks) for g in range(GROUPS)]

    def copy(source, turn, block, g):
        first, wide = pieces[turn]
        part = pl.ds(g * group, group)
        return pltpu.make_async_copy(
            source.at[block, part, pl.ds(first, wide)], outs[turn].at[block, part], sems.at[turn, block, g]
        )

    for index, source in enumerate(sources):

        @pl.when(which[0] == index)
        def start(source=source):
            for which_part in copies:
                copy(source, *which_part).start()

    @pl.when(which[0] < len(sources))
    def wait():
        for which_part in copies:
            copy(sources[0], *which_part).wait()


def in_hbm(value):
    return pltpu.with_memory_space_constraint(value, pltpu.HBM)


def pack(which, sources, pieces):
    blocks, depth, _, inner = sources[0].shape
    shapes = [jax.ShapeDtypeStruct((blocks, depth, wide, inner), sources[0].dtype) for _, wide in pieces]
    return pl.pallas_call(
        functools.partial(pack_kernel, pieces),
        in_specs=[pl.BlockSpec(memory_space=pltpu.SMEM)] + [pl.BlockSpec(memory_space=pl.ANY)] * len(sources),
        out_specs=[pl.BlockSpec(memory_space=pltpu.VMEM)] * len(pieces),
        scratch_shapes=[pltpu.SemaphoreType.DMA((len(pieces), blocks, GROUPS))],
        out_shape=shapes,
        compiler_params=pltpu.CompilerParams(vmem_limit_bytes=KERNEL_BYTES),
        cost_estimate=pl.CostEstimate(flops=0, bytes_accessed=1 << 20, transcendentals=0),
        name="pack_ranges",
    )(which, *sources)


def pair_kernel(slots, first, wide, parts, places, unread, rows_hbm, *refs):
    *refs, rows, held, total, row_sems, column_sems = refs
    sources, outs = refs[:-parts], refs[-parts:]
    blocks, depth, height, inner = rows.shape
    count = blocks * slots
    group = depth // GROUPS

    def row_copy(g):
        part = pl.ds(g * group, group)
        return pltpu.make_async_copy(rows_hbm.at[:, part], rows.at[:, part], row_sems.at[g])

    def column_copy(source, slot, g):
        part = pl.ds(g * group, group)
        start = first if source.shape[2] == height else 0
        return pltpu.make_async_copy(
            source.at[places[count + slot], part, pl.ds(start, wide)],
            held.at[slot // slots, part, pl.ds(slot % slots * wide, wide)],
            column_sems.at[slot, g],
        )

    for g in range(GROUPS):
        row_copy(g).start()
        for slot in range(count):
            for index, source in enumerate(sources):

                @pl.when(places[slot] == index)
                def fetch(source=source, slot=slot, g=g):
                    column_copy(source, slot, g).start()

    for g in range(GROUPS):
        row_copy(g).wait()
        for slot in range(count):

            @pl.when(places[slot] >= 0)
            def arrived(slot=slot, g=g):
                column_copy(sources[-1], slot, g).wait()

        for row in range(blocks):
            product = 0.0 if g == 0 else total[row]
            for p in range(g * group, (g + 1) * group):
                product += lax.dot_general(
                    held[row, p],
                    rows[row, p],
                    (((1,), (1,)), ((), ())),
                    preferred_element_type=jnp.float32,
                )
            total[row] = product

    parts = len(outs)
    lanes = outs[0].shape[2]
    span = height // parts
    fold = lanes // span
    for slot in range(count):
        start = slot % slots * wide
        block = jnp.where(places[slot] >= 0, total[slot // slots, start : start + wide], 0.0)
        left = slot % fold * span
        for mine in range(parts):

            @pl.when(places[2 * count] == mine)
            def write(slot=slot, block=block, left=left, mine=mine):
                for step, out in enumerate(outs):
                    part = (mine + step) % parts
                    out[slot // fold, :, left : left + span] = block[:, part * span : (part + 1) * span]


def pair_products(places, begun, rows, columns, piece, parts, slots):
    first, wide = piece
    blocks, depth, height, inner = rows.shape
    count = blocks * slots
    fold = LANES * parts // height if count % (LANES * parts // height) == 0 else 1
    shape = (count // fold, wide, height // parts * fold)
    return pl.pallas_call(
        functools.partial(pair_kernel, slots, first, wide, parts),
        in_specs=[pl.BlockSpec(memory_space=pltpu.SMEM)] + [pl.BlockSpec(memory_space=pl.ANY)]
        + [pl.BlockSpec(memory_space=pl.ANY)] * (1 + len(columns)),
        out_specs=[pl.BlockSpec(memory_space=pltpu.VMEM)] * parts,
        scratch_shapes=[
            pltpu.VMEM(rows.shape, rows.dtype),
            pltpu.VMEM((blocks, depth, slots * wide, inner), rows.dtype),
            pltpu.VMEM((blocks, slots * wide, height), jnp.float32),
            pltpu.SemaphoreType.DMA((GROUPS,)),
            pltpu.SemaphoreType.DMA((count, GROUPS)),
        ],
        out_shape=[jax.ShapeDtypeStruct(shape, jnp.float32)] * parts,
        compiler_params=pltpu.CompilerParams(vmem_limit_bytes=KERNEL_BYTES),
        cost_estimate=pl.CostEstimate(flops=0, bytes_accessed=1 << 20, transcendentals=0),
        name="pair_products",
    )(places, begun, *(in_hbm(a) if a.shape == rows.shape else a for a in (rows, *columns)))


def sum_kernel(parts, *refs):
    *terms, out = refs
    pairs, _, lanes = terms[0].shape
    span = out.shape[1]
    for pair in range(pairs):
        sums = [sum(term[pair] for term in terms[k : k + parts]) for k in range(0, len(terms), parts)]
        turned = jnp.concatenate(sums, axis=0).T
        for side in range(lanes // span):
            out[pair * (lanes // span) + side] = turned[side * span : (side + 1) * span]


def mark_kernel(value, out):
    out[...] = jnp.zeros_like(out)


def mark(value, flops=MARK_FLOPS):
    return pl.pallas_call(
        mark_kernel,
        in_specs=[pl.BlockSpec(memory_space=pl.ANY)],
        out_specs=pl.BlockSpec(memory_space=pltpu.VMEM),
        out_shape=jax.ShapeDtypeStruct((8, LANES), jnp.float32),
        compiler_params=pltpu.CompilerParams(vmem_limit_bytes=1 << 20),
        cost_estimate=pl.CostEstimate(flops=flops, bytes_accessed=1024, transcendentals=0),
        name="mark",
    )(value)


def squares(factors, pair_cols, pair_count):
    blocks, _, height, _ = factors.shape
    slots = pair_cols.shape[1]
    devices = lax.axis_size("ao")
    parts = lax.axis_size("aux")
    chips = devices // 2
    me = lax.axis_index("ao")
    core = lax.rem(me, 2)
    even = lax.rem(me, 4) < 2

    to_core_0 = [(2 * c + 1, 2 * c) for c in range(chips)]
    to_core_1 = [(2 * c, 2 * c + 1) for c in range(chips)]
    early, late = [], []
    for c in range(0, chips, 2):
        across = (c + 2) % chips
        early += [(2 * across, 2 * c), (2 * c + 3, 2 * c + 1), (2 * across + 1, 2 * c + 3)]
        late += [(2 * c, 2 * c + 2), (2 * c + 2, 2 * c), (2 * across + 3, 2 * c + 3)]

    relative = jnp.mod(pair_cols - me * blocks, devices * blocks)
    slab = relative // blocks
    first_core = jnp.where(slab == 2, 4, jnp.where(slab == 3, 3, slab))
    second_core = jnp.where(slab == 1, 5, jnp.where(slab == 2, 2, jnp.where(even, 3, 4)))
    source = jnp.where((core == 0) | (slab == 0), first_core, second_core)
    live = lax.broadcasted_iota(jnp.int32, (blocks, slots), 1) < pair_count[:, None]
    places = jnp.concatenate([jnp.where(live, source, -1).reshape(-1), lax.rem(relative, blocks).reshape(-1)])
    places = jnp.concatenate([places, lax.axis_index("aux").astype(jnp.int32).reshape(1)])
    which = jnp.where(even, 3 * core, 1 + core).astype(jnp.int32).reshape(1)

    one = lax.ppermute(factors, "ao", early)
    mate = lax.ppermute(after(factors, places), "ao", to_core_0 + to_core_1[1::2])
    one_mate = lax.ppermute(one, "ao", to_core_0 + to_core_1[::2])
    senders = [one, in_hbm(factors), mate]
    sent = pack(which, senders, PIECES[:1])
    sent += pack(after(which, places, *sent), senders, PIECES[1:])
    twos, made, terms, marks = [], [], [], [mark(sent[-1], 10**12)]
    for turn, piece in enumerate(PIECES):
        twos.append(lax.ppermute(after(sent[turn], *made[: max(turn - 1, 0)][-1:]), "ao", late))
        earlier = terms[-parts // 2 : 1 - parts // 2] if turn else []
        two_mate = lax.ppermute(after(twos[turn], marks[turn], *earlier), "ao", to_core_1)
        columns = [factors, mate, one, one_mate, twos[turn], two_mate]
        products = pair_products(places, marks[turn], factors, columns, piece, parts, slots)
        made.append(products[0])
        if turn + 1 < len(PIECES):
            marks.append(mark(products[0]))
        terms.append(products[0])
        others = [t for k, t in enumerate(terms) if k // parts == turn - 1 and k % parts]
        for step in range(1, parts):
            terms.append(lax.ppermute(after(products[step], *others), "aux", [(z, (z + step) % parts) for z in range(parts)]))
    out = pl.pallas_call(
        functools.partial(sum_kernel, parts),
        out_shape=jax.ShapeDtypeStruct((blocks * slots, height // parts, height), jnp.float32),
        compiler_params=pltpu.CompilerParams(vmem_limit_bytes=KERNEL_BYTES),
        name="sum_terms",
    )(*terms)
    return out.reshape(blocks, slots, height // parts, height)


def after(value, *others):
    return lax.optimization_barrier((value, *others))[0]


def from_behind(value, axis, steps):
    count = lax.axis_size(axis)
    pairs = [(source, (source + steps) % count) for source in range(count)]
    return lax.ppermute(value, axis, pairs)


def ring(factors, pair_cols, pair_count):
    blocks_dev = factors.shape[0]
    slot_total = pair_cols.shape[1]
    devices = lax.axis_size("ao")

    def advance(carry, unused):
        arrived = from_behind(carry, "ao", -1)
        return (arrived, arrived)

    last_block, received = lax.scan(advance, factors, None, length=devices // 2 - 1)
    resident = jnp.concatenate([factors, received.reshape((-1,) + factors.shape[1:])], axis=0)
    offset = lax.axis_index("ao") * blocks_dev
    slot_index = jnp.mod(pair_cols - offset, devices * blocks_dev)
    columns = jnp.take(resident, slot_index.reshape(-1), axis=0)
    columns = columns.reshape((blocks_dev, slot_total) + factors.shape[1:])
    partial_value = jnp.einsum(
        "apri,aspci->asrc", factors, columns, preferred_element_type=jnp.float32
    )
    active = lax.broadcasted_iota(jnp.int32, (blocks_dev, slot_total), 1) < pair_count[:, None]
    partial_value = jnp.where(active[:, :, None, None], partial_value, 0.0)
    return lax.psum_scatter(partial_value, "aux", scatter_dimension=2, tiled=True)


def solution(mesh):
    return jax.shard_map(
        squares if mesh.shape["ao"] == 8 else ring,
        mesh=mesh,
        in_specs=(P("ao", "aux", None, None), P("ao", None), P("ao")),
        out_specs=P("ao", None, "aux", None),
        check_vma=False,
    )
```

```python
import functools

import jax
import jax.numpy as jnp
from jax import lax
from jax.experimental import pallas as pl
from jax.experimental.pallas import tpu as pltpu
from jax.sharding import PartitionSpec as P

LANES = 128
PIECES = ((0, 48), (48, 96), (144, 112))
GROUPS = 4
KERNEL_BYTES = 14 << 20
MARK_FLOPS = 10**6


def pack_kernel(pieces, which, *refs):
    sources, outs, sems = refs[: -len(pieces) - 1], refs[-len(pieces) - 1 : -1], refs[-1]
    blocks, depth = outs[0].shape[:2]
    group = depth // GROUPS
    copies = [(turn, block, g) for turn in range(len(pieces)) for block in range(blocks) for g in range(GROUPS)]

    def copy(source, turn, block, g):
        first, wide = pieces[turn]
        part = pl.ds(g * group, group)
        return pltpu.make_async_copy(
            source.at[block, part, pl.ds(first, wide)], outs[turn].at[block, part], sems.at[turn, block, g]
        )

    for index, source in enumerate(sources):

        @pl.when(which[0] == index)
        def start(source=source):
            for which_part in copies:
                copy(source, *which_part).start()

    @pl.when(which[0] < len(sources))
    def wait():
        for which_part in copies:
            copy(sources[0], *which_part).wait()


def in_hbm(value):
    return pltpu.with_memory_space_constraint(value, pltpu.HBM)


def pack(which, sources, pieces):
    blocks, depth, _, inner = sources[0].shape
    shapes = [jax.ShapeDtypeStruct((blocks, depth, wide, inner), sources[0].dtype) for _, wide in pieces]
    return pl.pallas_call(
        functools.partial(pack_kernel, pieces),
        in_specs=[pl.BlockSpec(memory_space=pltpu.SMEM)] + [pl.BlockSpec(memory_space=pl.ANY)] * len(sources),
        out_specs=[pl.BlockSpec(memory_space=pltpu.VMEM)] * len(pieces),
        scratch_shapes=[pltpu.SemaphoreType.DMA((len(pieces), blocks, GROUPS))],
        out_shape=shapes,
        compiler_params=pltpu.CompilerParams(vmem_limit_bytes=KERNEL_BYTES),
        cost_estimate=pl.CostEstimate(flops=0, bytes_accessed=1 << 20, transcendentals=0),
        name="pack_ranges",
    )(which, *sources)


def pair_kernel(slots, first, wide, parts, places, unread, rows_hbm, *refs):
    *refs, rows, held, total, row_sems, column_sems = refs
    sources, outs = refs[:-parts], refs[-parts:]
    blocks, depth, height, inner = rows.shape
    count = blocks * slots
    group = depth // GROUPS

    def row_copy(g):
        part = pl.ds(g * group, group)
        return pltpu.make_async_copy(rows_hbm.at[:, part], rows.at[:, part], row_sems.at[g])

    def column_copy(source, slot, g):
        part = pl.ds(g * group, group)
        start = first if source.shape[2] == height else 0
        return pltpu.make_async_copy(
            source.at[places[count + slot], part, pl.ds(start, wide)],
            held.at[slot // slots, part, pl.ds(slot % slots * wide, wide)],
            column_sems.at[slot, g],
        )

    for g in range(GROUPS):
        row_copy(g).start()
        for slot in range(count):
            for index, source in enumerate(sources):

                @pl.when(places[slot] == index)
                def fetch(source=source, slot=slot, g=g):
                    column_copy(source, slot, g).start()

    for g in range(GROUPS):
        row_copy(g).wait()
        for slot in range(count):

            @pl.when(places[slot] >= 0)
            def arrived(slot=slot, g=g):
                column_copy(sources[-1], slot, g).wait()

        for row in range(blocks):
            product = 0.0 if g == 0 else total[row]
            for p in range(g * group, (g + 1) * group):
                product += lax.dot_general(
                    held[row, p],
                    rows[row, p],
                    (((1,), (1,)), ((), ())),
                    preferred_element_type=jnp.float32,
                )
            total[row] = product

    parts = len(outs)
    lanes = outs[0].shape[2]
    span = height // parts
    fold = lanes // span
    for slot in range(count):
        start = slot % slots * wide
        block = jnp.where(places[slot] >= 0, total[slot // slots, start : start + wide], 0.0)
        left = slot % fold * span
        for mine in range(parts):

            @pl.when(places[2 * count] == mine)
            def write(slot=slot, block=block, left=left, mine=mine):
                for step, out in enumerate(outs):
                    part = (mine + step) % parts
                    out[slot // fold, :, left : left + span] = block[:, part * span : (part + 1) * span]


def pair_products(places, begun, rows, columns, piece, parts, slots):
    first, wide = piece
    blocks, depth, height, inner = rows.shape
    count = blocks * slots
    fold = LANES * parts // height if count % (LANES * parts // height) == 0 else 1
    shape = (count // fold, wide, height // parts * fold)
    return pl.pallas_call(
        functools.partial(pair_kernel, slots, first, wide, parts),
        in_specs=[pl.BlockSpec(memory_space=pltpu.SMEM)] + [pl.BlockSpec(memory_space=pl.ANY)]
        + [pl.BlockSpec(memory_space=pl.ANY)] * (1 + len(columns)),
        out_specs=[pl.BlockSpec(memory_space=pltpu.VMEM)] * parts,
        scratch_shapes=[
            pltpu.VMEM(rows.shape, rows.dtype),
            pltpu.VMEM((blocks, depth, slots * wide, inner), rows.dtype),
            pltpu.VMEM((blocks, slots * wide, height), jnp.float32),
            pltpu.SemaphoreType.DMA((GROUPS,)),
            pltpu.SemaphoreType.DMA((count, GROUPS)),
        ],
        out_shape=[jax.ShapeDtypeStruct(shape, jnp.float32)] * parts,
        compiler_params=pltpu.CompilerParams(vmem_limit_bytes=KERNEL_BYTES),
        cost_estimate=pl.CostEstimate(flops=0, bytes_accessed=1 << 20, transcendentals=0),
        name="pair_products",
    )(places, begun, *(in_hbm(a) if a.shape == rows.shape else a for a in (rows, *columns)))


def sum_kernel(parts, *refs):
    *terms, out = refs
    pairs, _, lanes = terms[0].shape
    span = out.shape[1]
    for pair in range(pairs):
        sums = [sum(term[pair] for term in terms[k : k + parts]) for k in range(0, len(terms), parts)]
        turned = jnp.concatenate(sums, axis=0).T
        for side in range(lanes // span):
            out[pair * (lanes // span) + side] = turned[side * span : (side + 1) * span]


def mark_kernel(value, out):
    out[...] = jnp.zeros_like(out)


def mark(value, flops=MARK_FLOPS):
    return pl.pallas_call(
        mark_kernel,
        in_specs=[pl.BlockSpec(memory_space=pl.ANY)],
        out_specs=pl.BlockSpec(memory_space=pltpu.VMEM),
        out_shape=jax.ShapeDtypeStruct((8, LANES), jnp.float32),
        compiler_params=pltpu.CompilerParams(vmem_limit_bytes=1 << 20),
        cost_estimate=pl.CostEstimate(flops=flops, bytes_accessed=1024, transcendentals=0),
        name="mark",
    )(value)


def squares(factors, pair_cols, pair_count):
    blocks, _, height, _ = factors.shape
    slots = pair_cols.shape[1]
    devices = lax.axis_size("ao")
    parts = lax.axis_size("aux")
    chips = devices // 2
    me = lax.axis_index("ao")
    core = lax.rem(me, 2)
    even = lax.rem(me, 4) < 2

    to_core_0 = [(2 * c + 1, 2 * c) for c in range(chips)]
    to_core_1 = [(2 * c, 2 * c + 1) for c in range(chips)]
    early, late = [], []
    for c in range(0, chips, 2):
        across = (c + 2) % chips
        early += [(2 * across, 2 * c), (2 * c + 3, 2 * c + 1), (2 * across + 1, 2 * c + 3)]
        late += [(2 * c, 2 * c + 2), (2 * c + 2, 2 * c), (2 * across + 3, 2 * c + 3)]

    relative = jnp.mod(pair_cols - me * blocks, devices * blocks)
    slab = relative // blocks
    first_core = jnp.where(slab == 2, 4, jnp.where(slab == 3, 3, slab))
    second_core = jnp.where(slab == 1, 5, jnp.where(slab == 2, 2, jnp.where(even, 3, 4)))
    source = jnp.where((core == 0) | (slab == 0), first_core, second_core)
    live = lax.broadcasted_iota(jnp.int32, (blocks, slots), 1) < pair_count[:, None]
    places = jnp.concatenate([jnp.where(live, source, -1).reshape(-1), lax.rem(relative, blocks).reshape(-1)])
    places = jnp.concatenate([places, lax.axis_index("aux").astype(jnp.int32).reshape(1)])

    one = lax.ppermute(factors, "ao", early)
    which = after(jnp.where(even, 3 * core, 1 + core).astype(jnp.int32).reshape(1), one)
    which = jnp.minimum(which, 3)
    mate = lax.ppermute(after(factors, places), "ao", to_core_0 + to_core_1[1::2])
    one_mate = lax.ppermute(one, "ao", to_core_0 + to_core_1[::2])
    senders = [one, in_hbm(factors), mate]
    sent = pack(which, senders, PIECES[:1])
    sent += pack(after(which, places, *sent), senders, PIECES[1:])
    twos, made, terms, marks = [], [], [], [mark(sent[-1], 10**12)]
    for turn, piece in enumerate(PIECES):
        twos.append(lax.ppermute(after(sent[turn], *made[: max(turn - 1, 0)][-1:]), "ao", late))
        earlier = terms[1 - parts : 2 - parts] if turn else []
        two_mate = lax.ppermute(after(twos[turn], marks[turn], *earlier), "ao", to_core_1)
        columns = [factors, mate, one, one_mate, twos[turn], two_mate]
        products = pair_products(places, marks[turn], factors, columns, piece, parts, slots)
        made.append(products[0])
        if turn + 1 < len(PIECES):
            marks.append(mark(products[0]))
        terms.append(products[0])
        others = [t for k, t in enumerate(terms) if k // parts == turn - 1 and k % parts]
        for step in range(1, parts):
            terms.append(lax.ppermute(after(products[step], *others), "aux", [(z, (z + step) % parts) for z in range(parts)]))
    out = pl.pallas_call(
        functools.partial(sum_kernel, parts),
        out_shape=jax.ShapeDtypeStruct((blocks * slots, height // parts, height), jnp.float32),
        compiler_params=pltpu.CompilerParams(vmem_limit_bytes=KERNEL_BYTES),
        name="sum_terms",
    )(*terms)
    return out.reshape(blocks, slots, height // parts, height)


def after(value, *others):
    return lax.optimization_barrier((value, *others))[0]


def from_behind(value, axis, steps):
    count = lax.axis_size(axis)
    pairs = [(source, (source + steps) % count) for source in range(count)]
    return lax.ppermute(value, axis, pairs)


def ring(factors, pair_cols, pair_count):
    blocks_dev = factors.shape[0]
    slot_total = pair_cols.shape[1]
    devices = lax.axis_size("ao")

    def advance(carry, unused):
        arrived = from_behind(carry, "ao", -1)
        return (arrived, arrived)

    last_block, received = lax.scan(advance, factors, None, length=devices // 2 - 1)
    resident = jnp.concatenate([factors, received.reshape((-1,) + factors.shape[1:])], axis=0)
    offset = lax.axis_index("ao") * blocks_dev
    slot_index = jnp.mod(pair_cols - offset, devices * blocks_dev)
    columns = jnp.take(resident, slot_index.reshape(-1), axis=0)
    columns = columns.reshape((blocks_dev, slot_total) + factors.shape[1:])
    partial_value = jnp.einsum(
        "apri,aspci->asrc", factors, columns, preferred_element_type=jnp.float32
    )
    active = lax.broadcasted_iota(jnp.int32, (blocks_dev, slot_total), 1) < pair_count[:, None]
    partial_value = jnp.where(active[:, :, None, None], partial_value, 0.0)
    return lax.psum_scatter(partial_value, "aux", scatter_dimension=2, tiled=True)


def solution(mesh):
    return jax.shard_map(
        squares if mesh.shape["ao"] == 8 else ring,
        mesh=mesh,
        in_specs=(P("ao", "aux", None, None), P("ao", None), P("ao")),
        out_specs=P("ao", None, "aux", None),
        check_vma=False,
    )
```

```python
import functools

import jax
import jax.numpy as jnp
from jax import lax
from jax.experimental import pallas as pl
from jax.experimental.pallas import tpu as pltpu
from jax.sharding import PartitionSpec as P

LANES = 128
PIECES = ((0, 48), (48, 96), (144, 112))
GROUPS = 4
KERNEL_BYTES = 14 << 20
MARK_FLOPS = 10**6


def pack_kernel(pieces, which, *refs):
    sources, outs, sems = refs[: -len(pieces) - 1], refs[-len(pieces) - 1 : -1], refs[-1]
    blocks, depth = outs[0].shape[:2]
    group = depth // GROUPS
    copies = [(turn, block, g) for turn in range(len(pieces)) for block in range(blocks) for g in range(GROUPS)]

    def copy(source, turn, block, g):
        first, wide = pieces[turn]
        part = pl.ds(g * group, group)
        return pltpu.make_async_copy(
            source.at[block, part, pl.ds(first, wide)], outs[turn].at[block, part], sems.at[turn, block, g]
        )

    for index, source in enumerate(sources):

        @pl.when(which[0] == index)
        def start(source=source):
            for which_part in copies:
                copy(source, *which_part).start()

    @pl.when(which[0] < len(sources))
    def wait():
        for which_part in copies:
            copy(sources[0], *which_part).wait()


def in_hbm(value):
    return pltpu.with_memory_space_constraint(value, pltpu.HBM)


def pack(which, sources, pieces):
    blocks, depth, _, inner = sources[0].shape
    shapes = [jax.ShapeDtypeStruct((blocks, depth, wide, inner), sources[0].dtype) for _, wide in pieces]
    return pl.pallas_call(
        functools.partial(pack_kernel, pieces),
        in_specs=[pl.BlockSpec(memory_space=pltpu.SMEM)] + [pl.BlockSpec(memory_space=pl.ANY)] * len(sources),
        out_specs=[pl.BlockSpec(memory_space=pltpu.VMEM)] * len(pieces),
        scratch_shapes=[pltpu.SemaphoreType.DMA((len(pieces), blocks, GROUPS))],
        out_shape=shapes,
        compiler_params=pltpu.CompilerParams(vmem_limit_bytes=KERNEL_BYTES),
        cost_estimate=pl.CostEstimate(flops=0, bytes_accessed=1 << 20, transcendentals=0),
        name="pack_ranges",
    )(which, *sources)


def pair_kernel(slots, first, wide, parts, places, unread, rows_hbm, *refs):
    *refs, rows, held, total, row_sems, column_sems = refs
    sources, outs = refs[:-parts], refs[-parts:]
    blocks, depth, height, inner = rows.shape
    count = blocks * slots
    group = depth // GROUPS

    def row_copy(g):
        part = pl.ds(g * group, group)
        return pltpu.make_async_copy(rows_hbm.at[:, part], rows.at[:, part], row_sems.at[g])

    def column_copy(source, slot, g):
        part = pl.ds(g * group, group)
        start = first if source.shape[2] == height else 0
        return pltpu.make_async_copy(
            source.at[places[count + slot], part, pl.ds(start, wide)],
            held.at[slot // slots, part, pl.ds(slot % slots * wide, wide)],
            column_sems.at[slot, g],
        )

    for g in range(GROUPS):
        row_copy(g).start()
        for slot in range(count):
            for index, source in enumerate(sources):

                @pl.when(places[slot] == index)
                def fetch(source=source, slot=slot, g=g):
                    column_copy(source, slot, g).start()

    for g in range(GROUPS):
        row_copy(g).wait()
        for slot in range(count):

            @pl.when(places[slot] >= 0)
            def arrived(slot=slot, g=g):
                column_copy(sources[-1], slot, g).wait()

        for row in range(blocks):
            product = 0.0 if g == 0 else total[row]
            for p in range(g * group, (g + 1) * group):
                product += lax.dot_general(
                    held[row, p],
                    rows[row, p],
                    (((1,), (1,)), ((), ())),
                    preferred_element_type=jnp.float32,
                )
            total[row] = product

    parts = len(outs)
    lanes = outs[0].shape[2]
    span = height // parts
    fold = lanes // span
    for slot in range(count):
        start = slot % slots * wide
        block = jnp.where(places[slot] >= 0, total[slot // slots, start : start + wide], 0.0)
        left = slot % fold * span
        for mine in range(parts):

            @pl.when(places[2 * count] == mine)
            def write(slot=slot, block=block, left=left, mine=mine):
                for step, out in enumerate(outs):
                    part = (mine + step) % parts
                    out[slot // fold, :, left : left + span] = block[:, part * span : (part + 1) * span]


def pair_products(places, begun, rows, columns, piece, parts, slots):
    first, wide = piece
    blocks, depth, height, inner = rows.shape
    count = blocks * slots
    fold = LANES * parts // height if count % (LANES * parts // height) == 0 else 1
    shape = (count // fold, wide, height // parts * fold)
    return pl.pallas_call(
        functools.partial(pair_kernel, slots, first, wide, parts),
        in_specs=[pl.BlockSpec(memory_space=pltpu.SMEM)] + [pl.BlockSpec(memory_space=pl.ANY)]
        + [pl.BlockSpec(memory_space=pl.ANY)] * (1 + len(columns)),
        out_specs=[pl.BlockSpec(memory_space=pltpu.VMEM)] * parts,
        scratch_shapes=[
            pltpu.VMEM(rows.shape, rows.dtype),
            pltpu.VMEM((blocks, depth, slots * wide, inner), rows.dtype),
            pltpu.VMEM((blocks, slots * wide, height), jnp.float32),
            pltpu.SemaphoreType.DMA((GROUPS,)),
            pltpu.SemaphoreType.DMA((count, GROUPS)),
        ],
        out_shape=[jax.ShapeDtypeStruct(shape, jnp.float32)] * parts,
        compiler_params=pltpu.CompilerParams(vmem_limit_bytes=KERNEL_BYTES),
        cost_estimate=pl.CostEstimate(flops=0, bytes_accessed=1 << 20, transcendentals=0),
        name="pair_products",
    )(places, begun, *(in_hbm(a) if a.shape == rows.shape else a for a in (rows, *columns)))


def sum_kernel(parts, *refs):
    *terms, out = refs
    pairs, _, lanes = terms[0].shape
    span = out.shape[1]
    for pair in range(pairs):
        sums = [sum(term[pair] for term in terms[k : k + parts]) for k in range(0, len(terms), parts)]
        turned = jnp.concatenate(sums, axis=0).T
        for side in range(lanes // span):
            out[pair * (lanes // span) + side] = turned[side * span : (side + 1) * span]


def mark_kernel(value, out):
    out[...] = jnp.zeros_like(out)


def mark(value, flops=MARK_FLOPS):
    return pl.pallas_call(
        mark_kernel,
        in_specs=[pl.BlockSpec(memory_space=pl.ANY)],
        out_specs=pl.BlockSpec(memory_space=pltpu.VMEM),
        out_shape=jax.ShapeDtypeStruct((8, LANES), jnp.float32),
        compiler_params=pltpu.CompilerParams(vmem_limit_bytes=1 << 20),
        cost_estimate=pl.CostEstimate(flops=flops, bytes_accessed=1024, transcendentals=0),
        name="mark",
    )(value)


def squares(factors, pair_cols, pair_count):
    blocks, _, height, _ = factors.shape
    slots = pair_cols.shape[1]
    devices = lax.axis_size("ao")
    parts = lax.axis_size("aux")
    chips = devices // 2
    me = lax.axis_index("ao")
    core = lax.rem(me, 2)
    even = lax.rem(me, 4) < 2

    to_core_0 = [(2 * c + 1, 2 * c) for c in range(chips)]
    to_core_1 = [(2 * c, 2 * c + 1) for c in range(chips)]
    early, late = [], []
    for c in range(0, chips, 2):
        across = (c + 2) % chips
        early += [(2 * across, 2 * c), (2 * c + 3, 2 * c + 1), (2 * across + 1, 2 * c + 3)]
        late += [(2 * c, 2 * c + 2), (2 * c + 2, 2 * c), (2 * across + 3, 2 * c + 3)]

    relative = jnp.mod(pair_cols - me * blocks, devices * blocks)
    slab = relative // blocks
    first_core = jnp.where(slab == 2, 4, jnp.where(slab == 3, 3, slab))
    second_core = jnp.where(slab == 1, 5, jnp.where(slab == 2, 2, jnp.where(even, 3, 4)))
    source = jnp.where((core == 0) | (slab == 0), first_core, second_core)
    live = lax.broadcasted_iota(jnp.int32, (blocks, slots), 1) < pair_count[:, None]
    places = jnp.concatenate([jnp.where(live, source, -1).reshape(-1), lax.rem(relative, blocks).reshape(-1)])
    places = jnp.concatenate([places, lax.axis_index("aux").astype(jnp.int32).reshape(1)])

    one = lax.ppermute(factors, "ao", early)
    which = after(jnp.where(even, 3 * core, 1 + core).astype(jnp.int32).reshape(1), one)
    which = jnp.minimum(which, 3)
    mate = lax.ppermute(after(factors, places), "ao", to_core_0 + to_core_1[1::2])
    one_mate = lax.ppermute(one, "ao", to_core_0 + to_core_1[::2])
    senders = [one, in_hbm(factors), mate]
    sent = pack(which, senders, PIECES[:1])
    sent += pack(after(which, places, *sent), senders, PIECES[1:])
    twos, made, terms, marks = [], [], [], [mark(sent[-1], 10**12)]
    for turn, piece in enumerate(PIECES):
        twos.append(lax.ppermute(after(sent[turn], *made[: max(turn - 1, 0)][-1:]), "ao", late))
        earlier = terms[1 - parts :: 2][: min(turn, 2)] if turn else []
        two_mate = lax.ppermute(after(twos[turn], marks[turn], *earlier), "ao", to_core_1)
        columns = [factors, mate, one, one_mate, twos[turn], two_mate]
        products = pair_products(places, marks[turn], factors, columns, piece, parts, slots)
        made.append(products[0])
        if turn + 1 < len(PIECES):
            marks.append(mark(products[0]))
        terms.append(products[0])
        others = [t for k, t in enumerate(terms) if k // parts == turn - 1 and k % parts]
        for step in range(1, parts):
            terms.append(lax.ppermute(after(products[step], *others), "aux", [(z, (z + step) % parts) for z in range(parts)]))
    out = pl.pallas_call(
        functools.partial(sum_kernel, parts),
        out_shape=jax.ShapeDtypeStruct((blocks * slots, height // parts, height), jnp.float32),
        compiler_params=pltpu.CompilerParams(vmem_limit_bytes=KERNEL_BYTES),
        name="sum_terms",
    )(*terms)
    return out.reshape(blocks, slots, height // parts, height)


def after(value, *others):
    return lax.optimization_barrier((value, *others))[0]


def from_behind(value, axis, steps):
    count = lax.axis_size(axis)
    pairs = [(source, (source + steps) % count) for source in range(count)]
    return lax.ppermute(value, axis, pairs)


def ring(factors, pair_cols, pair_count):
    blocks_dev = factors.shape[0]
    slot_total = pair_cols.shape[1]
    devices = lax.axis_size("ao")

    def advance(carry, unused):
        arrived = from_behind(carry, "ao", -1)
        return (arrived, arrived)

    last_block, received = lax.scan(advance, factors, None, length=devices // 2 - 1)
    resident = jnp.concatenate([factors, received.reshape((-1,) + factors.shape[1:])], axis=0)
    offset = lax.axis_index("ao") * blocks_dev
    slot_index = jnp.mod(pair_cols - offset, devices * blocks_dev)
    columns = jnp.take(resident, slot_index.reshape(-1), axis=0)
    columns = columns.reshape((blocks_dev, slot_total) + factors.shape[1:])
    partial_value = jnp.einsum(
        "apri,aspci->asrc", factors, columns, preferred_element_type=jnp.float32
    )
    active = lax.broadcasted_iota(jnp.int32, (blocks_dev, slot_total), 1) < pair_count[:, None]
    partial_value = jnp.where(active[:, :, None, None], partial_value, 0.0)
    return lax.psum_scatter(partial_value, "aux", scatter_dimension=2, tiled=True)


def solution(mesh):
    return jax.shard_map(
        squares if mesh.shape["ao"] == 8 else ring,
        mesh=mesh,
        in_specs=(P("ao", "aux", None, None), P("ao", None), P("ao")),
        out_specs=P("ao", None, "aux", None),
        check_vma=False,
    )
```

```python
import functools

import jax
import jax.numpy as jnp
from jax import lax
from jax.experimental import pallas as pl
from jax.experimental.pallas import tpu as pltpu
from jax.sharding import PartitionSpec as P

LANES = 128
PIECES = ((0, 48), (48, 96), (144, 112))
GROUPS = 4
KERNEL_BYTES = 10 << 20
MARK_FLOPS = 10**6


def pack_kernel(pieces, which, *refs):
    sources, outs, sems = refs[: -len(pieces) - 1], refs[-len(pieces) - 1 : -1], refs[-1]
    blocks, depth = outs[0].shape[:2]
    group = depth // GROUPS
    copies = [(turn, block, g) for turn in range(len(pieces)) for block in range(blocks) for g in range(GROUPS)]

    def copy(source, turn, block, g):
        first, wide = pieces[turn]
        part = pl.ds(g * group, group)
        return pltpu.make_async_copy(
            source.at[block, part, pl.ds(first, wide)], outs[turn].at[block, part], sems.at[turn, block, g]
        )

    for index, source in enumerate(sources):

        @pl.when(which[0] == index)
        def start(source=source):
            for which_part in copies:
                copy(source, *which_part).start()

    @pl.when(which[0] < len(sources))
    def wait():
        for which_part in copies:
            copy(sources[0], *which_part).wait()


def in_hbm(value):
    return pltpu.with_memory_space_constraint(value, pltpu.HBM)


def hold_kernel(source, out, sem):
    pltpu.async_copy(source, out, sem).wait()


def hold(value):
    return pl.pallas_call(
        hold_kernel,
        in_specs=[pl.BlockSpec(memory_space=pl.ANY)],
        out_specs=pl.BlockSpec(memory_space=pl.ANY),
        scratch_shapes=[pltpu.SemaphoreType.DMA],
        out_shape=pltpu.VMEM(value.shape, value.dtype),
        compiler_params=pltpu.CompilerParams(vmem_limit_bytes=1 << 20),
        name="hold_rows",
    )(in_hbm(value))


def pack(which, sources, pieces):
    blocks, depth, _, inner = sources[0].shape
    shapes = [jax.ShapeDtypeStruct((blocks, depth, wide, inner), sources[0].dtype) for _, wide in pieces]
    return pl.pallas_call(
        functools.partial(pack_kernel, pieces),
        in_specs=[pl.BlockSpec(memory_space=pltpu.SMEM)] + [pl.BlockSpec(memory_space=pl.ANY)] * len(sources),
        out_specs=[pl.BlockSpec(memory_space=pltpu.VMEM)] * len(pieces),
        scratch_shapes=[pltpu.SemaphoreType.DMA((len(pieces), blocks, GROUPS))],
        out_shape=shapes,
        compiler_params=pltpu.CompilerParams(vmem_limit_bytes=KERNEL_BYTES),
        cost_estimate=pl.CostEstimate(flops=0, bytes_accessed=1 << 20, transcendentals=0),
        name="pack_ranges",
    )(which, *sources)


def pair_kernel(slots, first, wide, parts, places, unread, rows, *refs):
    *refs, held, total, column_sems = refs
    sources, outs = refs[:-parts], refs[-parts:]
    blocks, depth, height, inner = rows.shape
    count = blocks * slots
    group = depth // GROUPS

    def column_copy(source, slot, g):
        part = pl.ds(g * group, group)
        start = first if source.shape[2] == height else 0
        return pltpu.make_async_copy(
            source.at[places[count + slot], part, pl.ds(start, wide)],
            held.at[slot // slots, part, pl.ds(slot % slots * wide, wide)],
            column_sems.at[slot, g],
        )

    for g in range(GROUPS):
        for slot in range(count):
            for index, source in enumerate(sources):

                @pl.when(places[slot] == index)
                def fetch(source=source, slot=slot, g=g):
                    column_copy(source, slot, g).start()

    for g in range(GROUPS):
        for slot in range(count):

            @pl.when(places[slot] >= 0)
            def arrived(slot=slot, g=g):
                column_copy(sources[-1], slot, g).wait()

        for row in range(blocks):
            product = 0.0 if g == 0 else total[row]
            for p in range(g * group, (g + 1) * group):
                product += lax.dot_general(
                    held[row, p],
                    rows[row, p],
                    (((1,), (1,)), ((), ())),
                    preferred_element_type=jnp.float32,
                )
            total[row] = product

    parts = len(outs)
    lanes = outs[0].shape[2]
    span = height // parts
    fold = lanes // span
    for slot in range(count):
        start = slot % slots * wide
        block = jnp.where(places[slot] >= 0, total[slot // slots, start : start + wide], 0.0)
        left = slot % fold * span
        for mine in range(parts):

            @pl.when(places[2 * count] == mine)
            def write(slot=slot, block=block, left=left, mine=mine):
                for step, out in enumerate(outs):
                    part = (mine + step) % parts
                    out[slot // fold, :, left : left + span] = block[:, part * span : (part + 1) * span]


def pair_products(places, begun, rows, columns, piece, parts, slots):
    first, wide = piece
    blocks, depth, height, inner = rows.shape
    count = blocks * slots
    fold = LANES * parts // height if count % (LANES * parts // height) == 0 else 1
    shape = (count // fold, wide, height // parts * fold)
    return pl.pallas_call(
        functools.partial(pair_kernel, slots, first, wide, parts),
        in_specs=[pl.BlockSpec(memory_space=pltpu.SMEM)] + [pl.BlockSpec(memory_space=pl.ANY), pl.BlockSpec(memory_space=pltpu.VMEM)]
        + [pl.BlockSpec(memory_space=pl.ANY)] * len(columns),
        out_specs=[pl.BlockSpec(memory_space=pltpu.VMEM)] * parts,
        scratch_shapes=[
            pltpu.VMEM((blocks, depth, slots * wide, inner), rows.dtype),
            pltpu.VMEM((blocks, slots * wide, height), jnp.float32),
            pltpu.SemaphoreType.DMA((count, GROUPS)),
        ],
        out_shape=[jax.ShapeDtypeStruct(shape, jnp.float32)] * parts,
        compiler_params=pltpu.CompilerParams(vmem_limit_bytes=KERNEL_BYTES),
        cost_estimate=pl.CostEstimate(flops=0, bytes_accessed=1 << 20, transcendentals=0),
        name="pair_products",
    )(
        places,
        begun,
        pltpu.with_memory_space_constraint(rows, pltpu.VMEM),
        *(in_hbm(a) if a.shape == rows.shape else a for a in columns),
    )


def sum_kernel(parts, *refs):
    *terms, out = refs
    pairs, _, lanes = terms[0].shape
    span = out.shape[1]
    for pair in range(pairs):
        sums = [sum(term[pair] for term in terms[k : k + parts]) for k in range(0, len(terms), parts)]
        turned = jnp.concatenate(sums, axis=0).T
        for side in range(lanes // span):
            out[pair * (lanes // span) + side] = turned[side * span : (side + 1) * span]


def mark_kernel(value, out):
    out[...] = jnp.zeros_like(out)


def mark(value, flops=MARK_FLOPS):
    return pl.pallas_call(
        mark_kernel,
        in_specs=[pl.BlockSpec(memory_space=pl.ANY)],
        out_specs=pl.BlockSpec(memory_space=pltpu.VMEM),
        out_shape=jax.ShapeDtypeStruct((8, LANES), jnp.float32),
        compiler_params=pltpu.CompilerParams(vmem_limit_bytes=1 << 20),
        cost_estimate=pl.CostEstimate(flops=flops, bytes_accessed=1024, transcendentals=0),
        name="mark",
    )(value)


def squares(factors, pair_cols, pair_count):
    blocks, _, height, _ = factors.shape
    slots = pair_cols.shape[1]
    devices = lax.axis_size("ao")
    parts = lax.axis_size("aux")
    chips = devices // 2
    me = lax.axis_index("ao")
    core = lax.rem(me, 2)
    even = lax.rem(me, 4) < 2

    to_core_0 = [(2 * c + 1, 2 * c) for c in range(chips)]
    to_core_1 = [(2 * c, 2 * c + 1) for c in range(chips)]
    early, late = [], []
    for c in range(0, chips, 2):
        across = (c + 2) % chips
        early += [(2 * across, 2 * c), (2 * c + 3, 2 * c + 1), (2 * across + 1, 2 * c + 3)]
        late += [(2 * c, 2 * c + 2), (2 * c + 2, 2 * c), (2 * across + 3, 2 * c + 3)]

    relative = jnp.mod(pair_cols - me * blocks, devices * blocks)
    slab = relative // blocks
    first_core = jnp.where(slab == 2, 4, jnp.where(slab == 3, 3, slab))
    second_core = jnp.where(slab == 1, 5, jnp.where(slab == 2, 2, jnp.where(even, 3, 4)))
    source = jnp.where((core == 0) | (slab == 0), first_core, second_core)
    live = lax.broadcasted_iota(jnp.int32, (blocks, slots), 1) < pair_count[:, None]
    places = jnp.concatenate([jnp.where(live, source, -1).reshape(-1), lax.rem(relative, blocks).reshape(-1)])
    places = jnp.concatenate([places, lax.axis_index("aux").astype(jnp.int32).reshape(1)])

    one = lax.ppermute(factors, "ao", early)
    which = after(jnp.where(even, 3 * core, 1 + core).astype(jnp.int32).reshape(1), one)
    which = jnp.minimum(which, 3)
    mate = lax.ppermute(after(factors, places), "ao", to_core_0 + to_core_1[1::2])
    one_mate = lax.ppermute(one, "ao", to_core_0 + to_core_1[::2])
    rows = hold(after(factors, mate))
    senders = [one, in_hbm(factors), mate]
    sent = pack(which, senders, PIECES[:1])
    sent += pack(after(which, places, *sent), senders, PIECES[1:])
    twos, made, terms, marks = [], [], [], [mark(sent[-1], 10**12)]
    for turn, piece in enumerate(PIECES):
        twos.append(lax.ppermute(after(sent[turn], *made[: max(turn - 1, 0)][-1:]), "ao", late))
        earlier = terms[1 - parts : 2 - parts] if turn else []
        two_mate = lax.ppermute(after(twos[turn], marks[turn], *earlier), "ao", to_core_1)
        columns = [factors, mate, one, one_mate, twos[turn], two_mate]
        products = pair_products(places, marks[turn], rows, columns, piece, parts, slots)
        made.append(products[0])
        if turn + 1 < len(PIECES):
            marks.append(mark(products[0]))
        terms.append(products[0])
        others = [t for k, t in enumerate(terms) if k // parts == turn - 1 and k % parts]
        for step in range(1, parts):
            terms.append(lax.ppermute(after(products[step], *others), "aux", [(z, (z + step) % parts) for z in range(parts)]))
    out = pl.pallas_call(
        functools.partial(sum_kernel, parts),
        out_shape=jax.ShapeDtypeStruct((blocks * slots, height // parts, height), jnp.float32),
        compiler_params=pltpu.CompilerParams(vmem_limit_bytes=KERNEL_BYTES),
        name="sum_terms",
    )(*terms)
    return out.reshape(blocks, slots, height // parts, height)


def after(value, *others):
    return lax.optimization_barrier((value, *others))[0]


def from_behind(value, axis, steps):
    count = lax.axis_size(axis)
    pairs = [(source, (source + steps) % count) for source in range(count)]
    return lax.ppermute(value, axis, pairs)


def ring(factors, pair_cols, pair_count):
    blocks_dev = factors.shape[0]
    slot_total = pair_cols.shape[1]
    devices = lax.axis_size("ao")

    def advance(carry, unused):
        arrived = from_behind(carry, "ao", -1)
        return (arrived, arrived)

    last_block, received = lax.scan(advance, factors, None, length=devices // 2 - 1)
    resident = jnp.concatenate([factors, received.reshape((-1,) + factors.shape[1:])], axis=0)
    offset = lax.axis_index("ao") * blocks_dev
    slot_index = jnp.mod(pair_cols - offset, devices * blocks_dev)
    columns = jnp.take(resident, slot_index.reshape(-1), axis=0)
    columns = columns.reshape((blocks_dev, slot_total) + factors.shape[1:])
    partial_value = jnp.einsum(
        "apri,aspci->asrc", factors, columns, preferred_element_type=jnp.float32
    )
    active = lax.broadcasted_iota(jnp.int32, (blocks_dev, slot_total), 1) < pair_count[:, None]
    partial_value = jnp.where(active[:, :, None, None], partial_value, 0.0)
    return lax.psum_scatter(partial_value, "aux", scatter_dimension=2, tiled=True)


def solution(mesh):
    return jax.shard_map(
        squares if mesh.shape["ao"] == 8 else ring,
        mesh=mesh,
        in_specs=(P("ao", "aux", None, None), P("ao", None), P("ao")),
        out_specs=P("ao", None, "aux", None),
        check_vma=False,
    )
```

```python
import functools

import jax
import jax.numpy as jnp
from jax import lax
from jax.experimental import pallas as pl
from jax.experimental.pallas import tpu as pltpu
from jax.sharding import PartitionSpec as P

LANES = 128
PIECES = ((0, 48), (48, 96), (144, 112))
GROUPS = 4
KERNEL_BYTES = 10 << 20
MARK_FLOPS = 10**6


def pack_kernel(pieces, which, *refs):
    sources, outs, sems = refs[: -len(pieces) - 1], refs[-len(pieces) - 1 : -1], refs[-1]
    blocks, depth = outs[0].shape[:2]
    group = depth // GROUPS
    copies = [(turn, block, g) for turn in range(len(pieces)) for block in range(blocks) for g in range(GROUPS)]

    def copy(source, turn, block, g):
        first, wide = pieces[turn]
        part = pl.ds(g * group, group)
        return pltpu.make_async_copy(
            source.at[block, part, pl.ds(first, wide)], outs[turn].at[block, part], sems.at[turn, block, g]
        )

    for index, source in enumerate(sources):

        @pl.when(which[0] == index)
        def start(source=source):
            for which_part in copies:
                copy(source, *which_part).start()

    @pl.when(which[0] < len(sources))
    def wait():
        for which_part in copies:
            copy(sources[0], *which_part).wait()


def in_hbm(value):
    return pltpu.with_memory_space_constraint(value, pltpu.HBM)


def hold_kernel(source, out, sem):
    pltpu.async_copy(source, out, sem).wait()


def hold(value):
    return pl.pallas_call(
        hold_kernel,
        in_specs=[pl.BlockSpec(memory_space=pl.ANY)],
        out_specs=pl.BlockSpec(memory_space=pl.ANY),
        scratch_shapes=[pltpu.SemaphoreType.DMA],
        out_shape=pltpu.VMEM(value.shape, value.dtype),
        compiler_params=pltpu.CompilerParams(vmem_limit_bytes=1 << 20),
        name="hold_rows",
    )(in_hbm(value))


def pack(which, sources, pieces):
    blocks, depth, _, inner = sources[0].shape
    shapes = [jax.ShapeDtypeStruct((blocks, depth, wide, inner), sources[0].dtype) for _, wide in pieces]
    return pl.pallas_call(
        functools.partial(pack_kernel, pieces),
        in_specs=[pl.BlockSpec(memory_space=pltpu.SMEM)] + [pl.BlockSpec(memory_space=pl.ANY)] * len(sources),
        out_specs=[pl.BlockSpec(memory_space=pltpu.VMEM)] * len(pieces),
        scratch_shapes=[pltpu.SemaphoreType.DMA((len(pieces), blocks, GROUPS))],
        out_shape=shapes,
        compiler_params=pltpu.CompilerParams(vmem_limit_bytes=KERNEL_BYTES),
        cost_estimate=pl.CostEstimate(flops=0, bytes_accessed=1 << 20, transcendentals=0),
        name="pack_ranges",
    )(which, *sources)


def pair_kernel(slots, first, wide, parts, places, unread, rows, *refs):
    *refs, held, total, column_sems = refs
    sources, outs = refs[:-parts], refs[-parts:]
    blocks, depth, height, inner = rows.shape
    count = blocks * slots
    group = depth // GROUPS

    def column_copy(source, slot, g):
        part = pl.ds(g * group, group)
        start = first if source.shape[2] == height else 0
        return pltpu.make_async_copy(
            source.at[places[count + slot], part, pl.ds(start, wide)],
            held.at[slot // slots, part, pl.ds(slot % slots * wide, wide)],
            column_sems.at[slot, g],
        )

    for g in range(GROUPS):
        for slot in range(count):
            for index, source in enumerate(sources):

                @pl.when(places[slot] == index)
                def fetch(source=source, slot=slot, g=g):
                    column_copy(source, slot, g).start()

    for g in range(GROUPS):
        for slot in range(count):

            @pl.when(places[slot] >= 0)
            def arrived(slot=slot, g=g):
                column_copy(sources[-1], slot, g).wait()

        for row in range(blocks):
            product = 0.0 if g == 0 else total[row]
            for p in range(g * group, (g + 1) * group):
                product += lax.dot_general(
                    held[row, p],
                    rows[row, p],
                    (((1,), (1,)), ((), ())),
                    preferred_element_type=jnp.float32,
                )
            total[row] = product

    parts = len(outs)
    lanes = outs[0].shape[2]
    span = height // parts
    fold = lanes // span
    for slot in range(count):
        start = slot % slots * wide
        block = jnp.where(places[slot] >= 0, total[slot // slots, start : start + wide], 0.0)
        left = slot % fold * span
        for mine in range(parts):

            @pl.when(places[2 * count] == mine)
            def write(slot=slot, block=block, left=left, mine=mine):
                for step, out in enumerate(outs):
                    part = (mine + step) % parts
                    out[slot // fold, :, left : left + span] = block[:, part * span : (part + 1) * span]


def pair_products(places, begun, rows, columns, piece, parts, slots):
    first, wide = piece
    blocks, depth, height, inner = rows.shape
    count = blocks * slots
    fold = LANES * parts // height if count % (LANES * parts // height) == 0 else 1
    shape = (count // fold, wide, height // parts * fold)
    return pl.pallas_call(
        functools.partial(pair_kernel, slots, first, wide, parts),
        in_specs=[pl.BlockSpec(memory_space=pltpu.SMEM)] + [pl.BlockSpec(memory_space=pl.ANY), pl.BlockSpec(memory_space=pltpu.VMEM)]
        + [pl.BlockSpec(memory_space=pl.ANY)] * len(columns),
        out_specs=[pl.BlockSpec(memory_space=pltpu.VMEM)] * parts,
        scratch_shapes=[
            pltpu.VMEM((blocks, depth, slots * wide, inner), rows.dtype),
            pltpu.VMEM((blocks, slots * wide, height), jnp.float32),
            pltpu.SemaphoreType.DMA((count, GROUPS)),
        ],
        out_shape=[jax.ShapeDtypeStruct(shape, jnp.float32)] * parts,
        compiler_params=pltpu.CompilerParams(vmem_limit_bytes=KERNEL_BYTES),
        cost_estimate=pl.CostEstimate(flops=0, bytes_accessed=1 << 20, transcendentals=0),
        name="pair_products",
    )(
        places,
        begun,
        pltpu.with_memory_space_constraint(rows, pltpu.VMEM),
        *(in_hbm(a) if a.shape == rows.shape else a for a in columns),
    )


def sum_kernel(parts, *refs):
    *terms, out = refs
    pairs, _, lanes = terms[0].shape
    span = out.shape[1]
    for pair in range(pairs):
        sums = [sum(term[pair] for term in terms[k : k + parts]) for k in range(0, len(terms), parts)]
        turned = jnp.concatenate(sums, axis=0).T
        for side in range(lanes // span):
            out[pair * (lanes // span) + side] = turned[side * span : (side + 1) * span]


def mark_kernel(value, out):
    out[...] = jnp.zeros_like(out)


def mark(value, flops=MARK_FLOPS):
    return pl.pallas_call(
        mark_kernel,
        in_specs=[pl.BlockSpec(memory_space=pl.ANY)],
        out_specs=pl.BlockSpec(memory_space=pltpu.VMEM),
        out_shape=jax.ShapeDtypeStruct((8, LANES), jnp.float32),
        compiler_params=pltpu.CompilerParams(vmem_limit_bytes=1 << 20),
        cost_estimate=pl.CostEstimate(flops=flops, bytes_accessed=1024, transcendentals=0),
        name="mark",
    )(value)


def squares(factors, pair_cols, pair_count):
    blocks, _, height, _ = factors.shape
    slots = pair_cols.shape[1]
    devices = lax.axis_size("ao")
    parts = lax.axis_size("aux")
    chips = devices // 2
    me = lax.axis_index("ao")
    core = lax.rem(me, 2)
    even = lax.rem(me, 4) < 2

    to_core_0 = [(2 * c + 1, 2 * c) for c in range(chips)]
    to_core_1 = [(2 * c, 2 * c + 1) for c in range(chips)]
    early, late = [], []
    for c in range(0, chips, 2):
        across = (c + 2) % chips
        early += [(2 * across, 2 * c), (2 * c + 3, 2 * c + 1), (2 * across + 1, 2 * c + 3)]
        late += [(2 * c, 2 * c + 2), (2 * c + 2, 2 * c), (2 * across + 3, 2 * c + 3)]

    relative = jnp.mod(pair_cols - me * blocks, devices * blocks)
    slab = relative // blocks
    first_core = jnp.where(slab == 2, 4, jnp.where(slab == 3, 3, slab))
    second_core = jnp.where(slab == 1, 5, jnp.where(slab == 2, 2, jnp.where(even, 3, 4)))
    source = jnp.where((core == 0) | (slab == 0), first_core, second_core)
    live = lax.broadcasted_iota(jnp.int32, (blocks, slots), 1) < pair_count[:, None]
    places = jnp.concatenate([jnp.where(live, source, -1).reshape(-1), lax.rem(relative, blocks).reshape(-1)])
    places = jnp.concatenate([places, lax.axis_index("aux").astype(jnp.int32).reshape(1)])

    one = lax.ppermute(factors, "ao", early)
    which = after(jnp.where(even, 3 * core, 1 + core).astype(jnp.int32).reshape(1), one)
    which = jnp.minimum(which, 3)
    mate = lax.ppermute(after(factors, places), "ao", to_core_0 + to_core_1[1::2])
    one_mate = lax.ppermute(one, "ao", to_core_0 + to_core_1[::2])
    rows = hold(after(factors, mate))
    senders = [one, in_hbm(factors), mate]
    sent = pack(which, senders, PIECES[:1])
    sent += pack(after(which, places, *sent), senders, PIECES[1:])
    twos, made, terms, marks = [], [], [], [mark(sent[-1], 10**12)]
    for turn, piece in enumerate(PIECES):
        twos.append(lax.ppermute(after(sent[turn], *made[: max(turn - 1, 0)][-1:]), "ao", late))
        earlier = terms[1 - parts :: 2][: min(turn, 2)] if turn else []
        two_mate = lax.ppermute(after(twos[turn], marks[turn], *earlier), "ao", to_core_1)
        columns = [factors, mate, one, one_mate, twos[turn], two_mate]
        products = pair_products(places, marks[turn], rows, columns, piece, parts, slots)
        made.append(products[0])
        if turn + 1 < len(PIECES):
            marks.append(mark(products[0]))
        terms.append(products[0])
        others = [t for k, t in enumerate(terms) if k // parts == turn - 1 and k % parts]
        for step in range(1, parts):
            terms.append(lax.ppermute(after(products[step], *others), "aux", [(z, (z + step) % parts) for z in range(parts)]))
    out = pl.pallas_call(
        functools.partial(sum_kernel, parts),
        out_shape=jax.ShapeDtypeStruct((blocks * slots, height // parts, height), jnp.float32),
        compiler_params=pltpu.CompilerParams(vmem_limit_bytes=KERNEL_BYTES),
        name="sum_terms",
    )(*terms)
    return out.reshape(blocks, slots, height // parts, height)


def after(value, *others):
    return lax.optimization_barrier((value, *others))[0]


def from_behind(value, axis, steps):
    count = lax.axis_size(axis)
    pairs = [(source, (source + steps) % count) for source in range(count)]
    return lax.ppermute(value, axis, pairs)


def ring(factors, pair_cols, pair_count):
    blocks_dev = factors.shape[0]
    slot_total = pair_cols.shape[1]
    devices = lax.axis_size("ao")

    def advance(carry, unused):
        arrived = from_behind(carry, "ao", -1)
        return (arrived, arrived)

    last_block, received = lax.scan(advance, factors, None, length=devices // 2 - 1)
    resident = jnp.concatenate([factors, received.reshape((-1,) + factors.shape[1:])], axis=0)
    offset = lax.axis_index("ao") * blocks_dev
    slot_index = jnp.mod(pair_cols - offset, devices * blocks_dev)
    columns = jnp.take(resident, slot_index.reshape(-1), axis=0)
    columns = columns.reshape((blocks_dev, slot_total) + factors.shape[1:])
    partial_value = jnp.einsum(
        "apri,aspci->asrc", factors, columns, preferred_element_type=jnp.float32
    )
    active = lax.broadcasted_iota(jnp.int32, (blocks_dev, slot_total), 1) < pair_count[:, None]
    partial_value = jnp.where(active[:, :, None, None], partial_value, 0.0)
    return lax.psum_scatter(partial_value, "aux", scatter_dimension=2, tiled=True)


def solution(mesh):
    return jax.shard_map(
        squares if mesh.shape["ao"] == 8 else ring,
        mesh=mesh,
        in_specs=(P("ao", "aux", None, None), P("ao", None), P("ao")),
        out_specs=P("ao", None, "aux", None),
        check_vma=False,
    )
```

```python
import functools

import jax
import jax.numpy as jnp
from jax import lax
from jax.experimental import pallas as pl
from jax.experimental.pallas import tpu as pltpu
from jax.sharding import PartitionSpec as P

LANES = 128
PIECES = ((0, 48), (48, 96), (144, 112))
GROUPS = 4
KERNEL_BYTES = 10 << 20
MARK_FLOPS = 10**6


def pack_kernel(pieces, which, *refs):
    sources, outs, sems = refs[: -len(pieces) - 1], refs[-len(pieces) - 1 : -1], refs[-1]
    blocks, depth = outs[0].shape[:2]
    group = depth // GROUPS
    copies = [(turn, block, g) for turn in range(len(pieces)) for block in range(blocks) for g in range(GROUPS)]

    def copy(source, turn, block, g):
        first, wide = pieces[turn]
        part = pl.ds(g * group, group)
        return pltpu.make_async_copy(
            source.at[block, part, pl.ds(first, wide)], outs[turn].at[block, part], sems.at[turn, block, g]
        )

    for index, source in enumerate(sources):

        @pl.when(which[0] == index)
        def start(source=source):
            for which_part in copies:
                copy(source, *which_part).start()

    @pl.when(which[0] < len(sources))
    def wait():
        for which_part in copies:
            copy(sources[0], *which_part).wait()


def in_hbm(value):
    return pltpu.with_memory_space_constraint(value, pltpu.HBM)


def hold_kernel(source, out, sem):
    pltpu.async_copy(source, out, sem).wait()


def hold(value):
    return pl.pallas_call(
        hold_kernel,
        in_specs=[pl.BlockSpec(memory_space=pl.ANY)],
        out_specs=pl.BlockSpec(memory_space=pl.ANY),
        scratch_shapes=[pltpu.SemaphoreType.DMA],
        out_shape=pltpu.VMEM(value.shape, value.dtype),
        compiler_params=pltpu.CompilerParams(vmem_limit_bytes=1 << 20),
        name="hold_rows",
    )(in_hbm(value))


def pack(which, sources, pieces):
    blocks, depth, _, inner = sources[0].shape
    shapes = [jax.ShapeDtypeStruct((blocks, depth, wide, inner), sources[0].dtype) for _, wide in pieces]
    return pl.pallas_call(
        functools.partial(pack_kernel, pieces),
        in_specs=[pl.BlockSpec(memory_space=pltpu.SMEM)] + [pl.BlockSpec(memory_space=pl.ANY)] * len(sources),
        out_specs=[pl.BlockSpec(memory_space=pltpu.VMEM)] * len(pieces),
        scratch_shapes=[pltpu.SemaphoreType.DMA((len(pieces), blocks, GROUPS))],
        out_shape=shapes,
        compiler_params=pltpu.CompilerParams(vmem_limit_bytes=KERNEL_BYTES),
        cost_estimate=pl.CostEstimate(flops=0, bytes_accessed=1 << 20, transcendentals=0),
        name="pack_ranges",
    )(which, *sources)


def pair_kernel(slots, first, wide, parts, places, unread, rows, *refs):
    *refs, held, total, column_sems = refs
    sources, outs = refs[:-parts], refs[-parts:]
    blocks, depth, height, inner = rows.shape
    count = blocks * slots
    group = depth // GROUPS

    def column_copy(source, slot, g):
        part = pl.ds(g * group, group)
        start = first if source.shape[2] == height else 0
        return pltpu.make_async_copy(
            source.at[places[count + slot], part, pl.ds(start, wide)],
            held.at[slot // slots, part, pl.ds(slot % slots * wide, wide)],
            column_sems.at[slot, g],
        )

    for g in range(GROUPS):
        for slot in range(count):
            for index, source in enumerate(sources):

                @pl.when(places[slot] == index)
                def fetch(source=source, slot=slot, g=g):
                    column_copy(source, slot, g).start()

    for g in range(GROUPS):
        for slot in range(count):

            @pl.when(places[slot] >= 0)
            def arrived(slot=slot, g=g):
                column_copy(sources[-1], slot, g).wait()

        for row in range(blocks):
            product = 0.0 if g == 0 else total[row]
            for p in range(g * group, (g + 1) * group):
                product += lax.dot_general(
                    held[row, p],
                    rows[row, p],
                    (((1,), (1,)), ((), ())),
                    preferred_element_type=jnp.float32,
                )
            total[row] = product

    parts = len(outs)
    lanes = outs[0].shape[2]
    span = height // parts
    fold = lanes // span
    for slot in range(count):
        start = slot % slots * wide
        block = jnp.where(places[slot] >= 0, total[slot // slots, start : start + wide], 0.0)
        left = slot % fold * span
        for mine in range(parts):

            @pl.when(places[2 * count] == mine)
            def write(slot=slot, block=block, left=left, mine=mine):
                for step, out in enumerate(outs):
                    part = (mine + step) % parts
                    out[slot // fold, :, left : left + span] = block[:, part * span : (part + 1) * span]


def pair_products(places, begun, rows, columns, piece, parts, slots):
    first, wide = piece
    blocks, depth, height, inner = rows.shape
    count = blocks * slots
    fold = LANES * parts // height if count % (LANES * parts // height) == 0 else 1
    shape = (count // fold, wide, height // parts * fold)
    return pl.pallas_call(
        functools.partial(pair_kernel, slots, first, wide, parts),
        in_specs=[pl.BlockSpec(memory_space=pltpu.SMEM)] + [pl.BlockSpec(memory_space=pl.ANY), pl.BlockSpec(memory_space=pltpu.VMEM)]
        + [pl.BlockSpec(memory_space=pl.ANY)] * len(columns),
        out_specs=[pl.BlockSpec(memory_space=pltpu.VMEM)] * parts,
        scratch_shapes=[
            pltpu.VMEM((blocks, depth, slots * wide, inner), rows.dtype),
            pltpu.VMEM((blocks, slots * wide, height), jnp.float32),
            pltpu.SemaphoreType.DMA((count, GROUPS)),
        ],
        out_shape=[jax.ShapeDtypeStruct(shape, jnp.float32)] * parts,
        compiler_params=pltpu.CompilerParams(vmem_limit_bytes=KERNEL_BYTES),
        cost_estimate=pl.CostEstimate(flops=0, bytes_accessed=1 << 20, transcendentals=0),
        name="pair_products",
    )(
        places,
        begun,
        pltpu.with_memory_space_constraint(rows, pltpu.VMEM),
        *(in_hbm(a) if a.shape == rows.shape else a for a in columns),
    )


def sum_kernel(parts, *refs):
    *terms, out = refs
    pairs, _, lanes = terms[0].shape
    span = out.shape[1]
    for pair in range(pairs):
        sums = [sum(term[pair] for term in terms[k : k + parts]) for k in range(0, len(terms), parts)]
        turned = jnp.concatenate(sums, axis=0).T
        for side in range(lanes // span):
            out[pair * (lanes // span) + side] = turned[side * span : (side + 1) * span]


def mark_kernel(value, out):
    out[...] = jnp.zeros_like(out)


def mark(value, flops=MARK_FLOPS):
    return pl.pallas_call(
        mark_kernel,
        in_specs=[pl.BlockSpec(memory_space=pl.ANY)],
        out_specs=pl.BlockSpec(memory_space=pltpu.VMEM),
        out_shape=jax.ShapeDtypeStruct((8, LANES), jnp.float32),
        compiler_params=pltpu.CompilerParams(vmem_limit_bytes=1 << 20),
        cost_estimate=pl.CostEstimate(flops=flops, bytes_accessed=1024, transcendentals=0),
        name="mark",
    )(value)


def squares(factors, pair_cols, pair_count):
    blocks, _, height, _ = factors.shape
    slots = pair_cols.shape[1]
    devices = lax.axis_size("ao")
    parts = lax.axis_size("aux")
    chips = devices // 2
    me = lax.axis_index("ao")
    core = lax.rem(me, 2)
    even = lax.rem(me, 4) < 2

    to_core_0 = [(2 * c + 1, 2 * c) for c in range(chips)]
    to_core_1 = [(2 * c, 2 * c + 1) for c in range(chips)]
    early, late = [], []
    for c in range(0, chips, 2):
        across = (c + 2) % chips
        early += [(2 * across, 2 * c), (2 * c + 3, 2 * c + 1), (2 * across + 1, 2 * c + 3)]
        late += [(2 * c, 2 * c + 2), (2 * c + 2, 2 * c), (2 * across + 3, 2 * c + 3)]

    relative = jnp.mod(pair_cols - me * blocks, devices * blocks)
    slab = relative // blocks
    first_core = jnp.where(slab == 2, 4, jnp.where(slab == 3, 3, slab))
    second_core = jnp.where(slab == 1, 5, jnp.where(slab == 2, 2, jnp.where(even, 3, 4)))
    source = jnp.where((core == 0) | (slab == 0), first_core, second_core)
    live = lax.broadcasted_iota(jnp.int32, (blocks, slots), 1) < pair_count[:, None]
    places = jnp.concatenate([jnp.where(live, source, -1).reshape(-1), lax.rem(relative, blocks).reshape(-1)])
    places = jnp.concatenate([places, lax.axis_index("aux").astype(jnp.int32).reshape(1)])

    one = lax.ppermute(factors, "ao", early)
    which = after(jnp.where(even, 3 * core, 1 + core).astype(jnp.int32).reshape(1), one)
    which = jnp.minimum(which, 3)
    mate = lax.ppermute(after(factors, places), "ao", to_core_0 + to_core_1[1::2])
    one_mate = lax.ppermute(one, "ao", to_core_0 + to_core_1[::2])
    rows = hold(after(factors, mate))
    senders = [one, in_hbm(factors), mate]
    first, wide = PIECES[0]
    mine, mates, opposite = (lax.slice_in_dim(a, first, first + wide, axis=2) for a in (factors, mate, one))
    late_core = which[0] != 1
    sent = [jnp.where(even, opposite, jnp.where(late_core, mates, mine))]
    sent += pack(after(which, places, *sent), senders, PIECES[1:])
    twos, made, terms, marks = [], [], [], [mark(sent[-1], 10**12)]
    for turn, piece in enumerate(PIECES):
        twos.append(lax.ppermute(after(sent[turn], *made[: max(turn - 1, 0)][-1:]), "ao", late))
        earlier = terms[1 - parts : 2 - parts] if turn else []
        two_mate = lax.ppermute(after(twos[turn], marks[turn], *earlier), "ao", to_core_1)
        columns = [factors, mate, one, one_mate, twos[turn], two_mate]
        products = pair_products(places, marks[turn], rows, columns, piece, parts, slots)
        made.append(products[0])
        if turn + 1 < len(PIECES):
            marks.append(mark(products[0]))
        terms.append(products[0])
        others = [t for k, t in enumerate(terms) if k // parts == turn - 1 and k % parts]
        for step in range(1, parts):
            terms.append(lax.ppermute(after(products[step], *others), "aux", [(z, (z + step) % parts) for z in range(parts)]))
    out = pl.pallas_call(
        functools.partial(sum_kernel, parts),
        out_shape=jax.ShapeDtypeStruct((blocks * slots, height // parts, height), jnp.float32),
        compiler_params=pltpu.CompilerParams(vmem_limit_bytes=KERNEL_BYTES),
        name="sum_terms",
    )(*terms)
    return out.reshape(blocks, slots, height // parts, height)


def after(value, *others):
    return lax.optimization_barrier((value, *others))[0]


def from_behind(value, axis, steps):
    count = lax.axis_size(axis)
    pairs = [(source, (source + steps) % count) for source in range(count)]
    return lax.ppermute(value, axis, pairs)


def ring(factors, pair_cols, pair_count):
    blocks_dev = factors.shape[0]
    slot_total = pair_cols.shape[1]
    devices = lax.axis_size("ao")

    def advance(carry, unused):
        arrived = from_behind(carry, "ao", -1)
        return (arrived, arrived)

    last_block, received = lax.scan(advance, factors, None, length=devices // 2 - 1)
    resident = jnp.concatenate([factors, received.reshape((-1,) + factors.shape[1:])], axis=0)
    offset = lax.axis_index("ao") * blocks_dev
    slot_index = jnp.mod(pair_cols - offset, devices * blocks_dev)
    columns = jnp.take(resident, slot_index.reshape(-1), axis=0)
    columns = columns.reshape((blocks_dev, slot_total) + factors.shape[1:])
    partial_value = jnp.einsum(
        "apri,aspci->asrc", factors, columns, preferred_element_type=jnp.float32
    )
    active = lax.broadcasted_iota(jnp.int32, (blocks_dev, slot_total), 1) < pair_count[:, None]
    partial_value = jnp.where(active[:, :, None, None], partial_value, 0.0)
    return lax.psum_scatter(partial_value, "aux", scatter_dimension=2, tiled=True)


def solution(mesh):
    return jax.shard_map(
        squares if mesh.shape["ao"] == 8 else ring,
        mesh=mesh,
        in_specs=(P("ao", "aux", None, None), P("ao", None), P("ao")),
        out_specs=P("ao", None, "aux", None),
        check_vma=False,
    )
```
